32 devices in a mesh: row: 4 (over y, core), col: 8 (over z, x).
Axes of the slice: x: 2, y: 2, z: 4, core: 2. Of those that a mesh axis runs over, the one named last changes fastest.
Arguments:
- orbitals: bfloat16 [64, 8, 48, 2304], P(('row', 'col')), may hold values from -6 to 6
- potential_boxes: float32 [64, 48, 2304], P(('row', 'col')), may hold values from 0 to 2
- corners: int32 [64, 3], P(('row', 'col')), may hold values from 0 to 511, as said below
- signs: int32 [64], P(('row', 'col')), may hold values from -1 to 1, as said below
- counts: int32 [64], P(('row', 'col')), may hold values from 1 to 8, as said below
Outputs:
- filtered: bfloat16 [64, 8, 48, 2304], P(('row', 'col'))
- density: float32 [64, 64, 512], P('row', 'col')
- hartree: float32 [64, 64, 512], P('row', 'col')
The draws below stay inside these ranges and needn't reach their ends.
Inputs may be any that keep to these rules, and one draw needn't show every extreme that they name: `corners`: for fragment f held at index d = f // 2 of the row+col axis, with r = d // 8 and c = d % 8, the corner's first entry lies in [r * 16, (r + 1) * 16) and its second in [c * 8, (c + 1) * 8); the third is any cell below 512. Fragments 2 i and 2 i + 1 have the same corner. Each entry is -1 or 1; fragments 2 i and 2 i + 1 have opposite signs. Fragments 2 i and 2 i + 1 have equal counts; some device holds a fragment with 8 and some device one with 1.
All inputs are finite; a program needn't handle non-finite values.
Results may differ from the reference program's by a relative error of at most 0.001.
Values may be sent and summed in bfloat16 or wider, within the bound.
A program may use at most 128 MiB of HBM per device.

```python
import math
import jax
import jax.numpy as jnp
from jax import lax

B = 48
ORB = 8
DEGREE = 6
FRAG_DEV = 2
CX = 16
CY = 8
NZ = 512
FRAGS = 64
NX = 64
NY = 64


def draw_corners(key, part):
    columns = NY // CY
    pairs = FRAGS // 2
    owner = 2 * jnp.arange(pairs, dtype=jnp.int32) // FRAG_DEV
    keys = jax.random.split(jax.random.fold_in(key, 11), 3)
    xs = owner // columns * CX + jax.random.randint(keys[0], (pairs,), 0, CX)
    ys = owner % columns * CY + jax.random.randint(keys[1], (pairs,), 0, CY)
    zs = jax.random.randint(keys[2], (pairs,), 0, NZ)
    paired = jnp.stack([xs, ys, zs], axis=1).astype(jnp.int32)
    return jnp.repeat(paired, 2, axis=0).astype(jnp.int32)


def draw_signs(key, part):
    pairs = FRAGS // 2
    first = 2 * jax.random.randint(jax.random.fold_in(key, 5), (pairs,), 0, 2) - 1
    return jnp.stack([first, -first], axis=1).reshape(FRAGS).astype(jnp.int32)


def draw_counts(key, part):
    holders = FRAGS // FRAG_DEV
    per_holder = FRAG_DEV // 2
    keys = jax.random.split(jax.random.fold_in(key, 23), 4)
    ceiling = jax.random.randint(keys[0], (holders, 1), 1, ORB + 1)
    spread = jax.random.randint(keys[1], (holders, per_holder), 0, ORB)
    pair_counts = 1 + spread % ceiling
    full_holder = jax.random.randint(keys[2], (), 0, holders)
    single_holder = (full_holder + 1 + jax.random.randint(keys[3], (), 0, holders - 1)) % holders
    holder_rows = jnp.arange(holders, dtype=jnp.int32)[:, None]
    first_pair = (jnp.arange(per_holder, dtype=jnp.int32) == 0)[None, :]
    pair_counts = jnp.where((holder_rows == full_holder) & first_pair, ORB, pair_counts)
    pair_counts = jnp.where((holder_rows == single_holder) & first_pair, 1, pair_counts)
    return jnp.repeat(pair_counts.reshape(holders * per_holder), 2).astype(jnp.int32)


def draw_orbitals(key, part):
    field = jax.random.normal(jax.random.fold_in(key, 37), (FRAGS, ORB, B, B * B), jnp.float32)
    return jnp.clip(field, -6.0, 6.0).astype(jnp.bfloat16)


def draw_potential_boxes(key, part):
    return jax.random.uniform(jax.random.fold_in(key, 43), (FRAGS, B, B * B), jnp.float32, 0.0, 2.0)


def setup_inputs(seed: int = 0) -> dict:
    key_of = jax.random.split(jax.random.key(seed), 6)
    orbitals = draw_orbitals(jax.random.fold_in(key_of[5], 71), 0)
    potential_boxes = draw_potential_boxes(jax.random.fold_in(key_of[5], 71), 0)
    corners = draw_corners(jax.random.fold_in(key_of[5], 71), 0)
    signs = draw_signs(jax.random.fold_in(key_of[5], 71), 0)
    counts = draw_counts(jax.random.fold_in(key_of[5], 71), 0)
    return dict(orbitals=orbitals, potential_boxes=potential_boxes, corners=corners, signs=signs, counts=counts)


CENTER = 5.25
HALF_WIDTH = 3.75
SCREEN = 0.0025

def hamiltonian(field, potential):
    side = field.shape[0]
    zpos = lax.broadcasted_iota(jnp.int32, field.shape, 1) % side
    zero_row = jnp.zeros_like(field[:1])
    next_x = jnp.concatenate([field[1:], zero_row], 0)
    prev_x = jnp.concatenate([zero_row, field[:-1]], 0)
    zero_col = jnp.zeros_like(field[:, :1])
    next_z = jnp.concatenate([field[:, 1:], zero_col], 1)
    prev_z = jnp.concatenate([zero_col, field[:, :-1]], 1)
    next_z = jnp.where(zpos == side - 1, 0.0, next_z)
    prev_z = jnp.where(zpos == 0, 0.0, prev_z)
    zero_plane = jnp.zeros_like(field[:, :side])
    next_y = jnp.concatenate([field[:, side:], zero_plane], 1)
    prev_y = jnp.concatenate([zero_plane, field[:, :-side]], 1)
    beside = next_x + prev_x + next_z + prev_z + next_y + prev_y
    return (3.0 + potential) * field - 0.5 * beside

def chebyshev(start, potential):

    def shifted(field):
        return (hamiltonian(field, potential) - CENTER * field) / HALF_WIDTH
    previous = start
    current = shifted(start)
    for order in range(2, DEGREE + 1):
        previous, current = (current, 2.0 * shifted(current) - previous)
    scale = lax.rsqrt(jnp.mean(current * current) + 1e-06)
    return current * scale

def wave_square(length, positions):
    signed_index = jnp.where(positions <= length // 2, positions, positions - length).astype(jnp.float32)
    wave = signed_index * (2 * math.pi / length)
    return wave * wave

def one_fragment(items):
    orbital_set, potential, live_count = items
    result = jax.vmap(lambda single: chebyshev(single.astype(jnp.float32), potential))(orbital_set)
    live = (jnp.arange(ORB, dtype=jnp.int32) < live_count)[:, None, None]
    result = jnp.where(live, result, 0.0)
    return (result.astype(jnp.bfloat16), lax.optimization_barrier(jnp.sum(result * result, axis=0)))

def reference(orbitals, potential_boxes, corners, signs, counts):
    filtered, boxes = lax.map(one_fragment, (orbitals, potential_boxes, counts))
    signed = boxes * signs.astype(jnp.float32)[:, None, None]
    cubes = signed.reshape(FRAGS, B, B, B)
    padded = jnp.zeros((NX + B, NY + B, NZ + B), jnp.float32)

    def place(grid, item):
        cube, corner = item
        start = (corner[0], corner[1], corner[2])
        region = lax.dynamic_slice(grid, start, (B, B, B))
        return (lax.dynamic_update_slice(grid, region + cube, start), None)
    padded, _ = lax.scan(place, padded, (cubes, corners))
    grid = padded[:NX].at[:B].add(padded[NX:])
    grid = grid[:, :NY].at[:, :B].add(grid[:, NY:])
    density = grid[:, :, :NZ].at[:, :, :B].add(grid[:, :, NZ:])
    spectrum = jnp.fft.fftn(density)
    k_square = wave_square(NX, jnp.arange(NX, dtype=jnp.int32))[:, None, None] + wave_square(NY, jnp.arange(NY, dtype=jnp.int32))[None, :, None] + wave_square(NZ, jnp.arange(NZ, dtype=jnp.int32))[None, None, :]
    factor = jnp.where(k_square > 0, SCREEN / (k_square + SCREEN), 0.0)
    hartree = jnp.real(jnp.fft.ifftn(spectrum * factor)).astype(jnp.float32)
    return (filtered, density, hartree)
```

```python
import functools
import math

import jax
import jax.numpy as jnp
import ml_dtypes
import numpy as np
from jax import lax
from jax.experimental import pallas as pl
from jax.experimental.pallas import tpu as pltpu
from jax.sharding import PartitionSpec as P

CENTER = 5.25
HALF_WIDTH = 3.75
SCREEN = 0.0025
LANES = 128
HALF = 64
GROUP = 8
HIGHEST = lax.Precision.HIGHEST
BF16 = jnp.bfloat16
F32 = jnp.float32
TILES = ((0, 0), (1, 0), (1, 1), (2, 1), (2, 2), (3, 2))


def real_basis(length):
    m = np.arange(length)[:, None]
    n = np.arange(length)[None, :]
    angle = 2 * np.pi * ((m * n) % length) / length
    rows = np.where(m <= length // 2, np.cos(angle), np.sin(angle))
    weight = np.where((m == 0) | (2 * m == length), 1.0, 2.0) / length
    return rows * np.sqrt(weight)


def split_table(table):
    high = table.astype(np.float32).astype(ml_dtypes.bfloat16)
    low = (table - high.astype(np.float64)).astype(np.float32).astype(ml_dtypes.bfloat16)
    return high, low


def split2(value):
    high = value.astype(BF16)
    return high, (value - high.astype(F32)).astype(BF16)


def dot(a, b, dims=((1,), (0,))):
    return lax.dot_general(a, b, (dims, ((), ())), preferred_element_type=F32)


def dot3(a, b, dims=((1,), (0,))):
    return dot(a[0], b[0], dims) + (dot(a[0], b[1], dims) + dot(a[1], b[0], dims))


def move_matrix(pair, tile, side, inward):
    shape = (2 * LANES, 2 * LANES)
    boxed = lax.broadcasted_iota(jnp.int32, shape, 1 if inward else 0)
    flat = lax.broadcasted_iota(jnp.int32, shape, 0 if inward else 1)
    y = 2 * pair + boxed // LANES
    fragment = boxed % LANES // HALF
    z = boxed % HALF
    hit = (fragment == flat // LANES) & (z < side)
    hit = hit & (y * side + z == tile * LANES + flat % LANES)
    return jnp.where(hit, 1.0, 0.0).astype(BF16)


def filter_kernel(
    reach,
    mesh_sizes,
    own,
    corners_ref,
    signs_ref,
    counts_ref,
    orb_ref,
    pot_ref,
    out_ref,
    send_ref,
    even,
    odd,
    coef,
    moves,
    packed,
    slab,
    scales,
):
    _, orbs, side, _ = orb_ref.shape
    rows = orbs * side
    groups = side // GROUP
    lane = lax.broadcasted_iota(jnp.int32, (orbs, LANES), 1)
    for index, (pair, tile) in enumerate(TILES):
        moves[index] = move_matrix(pair, tile, side, True)
    for field in (even, odd):
        zeros = jnp.zeros((field.shape[1], LANES), F32)
        field[0] = zeros
        field[side + 1] = zeros
        edge = jnp.zeros((orbs, LANES), F32)

        def clear(y, carry):
            field[y, pl.ds(0, orbs), :] = edge
            field[y, pl.ds(orbs * (side + 1), orbs), :] = edge
            return carry

        lax.fori_loop(1, side + 1, clear, 0)

    def spread(parts):
        results = []
        for pair in range(GROUP // 2):
            total = None
            for index, (p, tile) in enumerate(TILES):
                if p == pair:
                    term = dot(parts[tile], moves[index])
                    total = term if total is None else total + term
            results.append(total)
        return results

    def load_group(g, carry):
        base = g * (GROUP * side)
        parts = []
        pot_parts = []
        for tile in range(3):
            cols = pl.ds(pl.multiple_of(base + tile * LANES, LANES), LANES)
            parts.append(
                jnp.concatenate([orb_ref[f, :, :, cols].reshape(rows, LANES) for f in range(2)], 1)
            )
            pot = jnp.concatenate([pot_ref[f, :, cols] for f in range(2)], 1)
            first = pot.astype(BF16)
            rest = pot - first.astype(F32)
            second = rest.astype(BF16)
            third = (rest - second.astype(F32)).astype(BF16)
            pot_parts.append(jnp.concatenate([first, second, third], 0))
        fields = spread(parts)
        pots = spread(pot_parts)
        for pair in range(GROUP // 2):
            for k in range(2):
                y = g * GROUP + 2 * pair + k
                cols = slice(k * LANES, (k + 1) * LANES)
                for orb in range(orbs):
                    even[y + 1, pl.ds(orbs + orb, side, stride=orbs), :] = fields[pair][
                        orb * side : (orb + 1) * side, cols
                    ]
                stack = pots[pair][:, cols]
                pot = (stack[:side] + stack[side : 2 * side]) + stack[2 * side :]
                coef[y] = (pot + (3.0 - CENTER)) * (2.0 / HALF_WIDTH)
        return carry

    lax.fori_loop(0, groups, load_group, 0)

    coupling = jnp.where(lane % HALF < side, 1.0 / HALF_WIDTH, 0.0).astype(F32)

    def step(now, other, first, last):
        def plane(y, total):
            squares = None
            before = now[y, pl.ds(0, orbs), :]
            here = now[y, pl.ds(orbs, orbs), :]
            for x in range(side):
                row = pl.ds(orbs * (x + 1), orbs)
                after = now[y, pl.ds(orbs * (x + 2), orbs), :]
                beside = (before + after) + (now[y - 1, row, :] + now[y + 1, row, :])
                beside = beside + (
                    pltpu.roll(here, 1, axis=1) + pltpu.roll(here, LANES - 1, axis=1)
                )
                result = coef[y - 1, pl.ds(x, 1), :] * here - coupling * beside
                result = 0.5 * result if first else result - other[y, row, :]
                other[y, row, :] = result
                if last:
                    square = result * result
                    squares = square if squares is None else squares + square
                before, here = here, after
            return total + squares if last else total

        return lax.fori_loop(1, side + 1, plane, jnp.zeros((orbs, LANES), F32))

    step(even, odd, True, False)
    step(odd, even, False, False)
    step(even, odd, False, False)
    step(odd, even, False, False)
    step(even, odd, False, False)
    total = step(odd, even, False, True)

    left = lane < HALF
    sums = jnp.where(
        left,
        jnp.sum(jnp.where(left, total, 0.0), axis=1, keepdims=True),
        jnp.sum(jnp.where(left, 0.0, total), axis=1, keepdims=True),
    )
    shifted = sums * (1.0 / side**3) + 1e-6
    scale = lax.rsqrt(shifted)
    scale = scale * (1.5 - 0.5 * shifted * scale * scale)
    live = lax.broadcasted_iota(jnp.int32, (orbs, LANES), 0) < jnp.where(
        left, counts_ref[0], counts_ref[1]
    )
    scales[...] = jnp.where(live, scale, 0.0)
    sign = jnp.where(left, signs_ref[0], signs_ref[1]).astype(F32)[:1]

    for index, (pair, tile) in enumerate(TILES):
        moves[index] = move_matrix(pair, tile, side, False)
    row_index, col_index = own()
    own_x = corners_ref[0, 0] - row_index * reach[2]
    own_y = corners_ref[0, 1] - col_index * reach[3]
    slab[...] = jnp.zeros_like(slab)
    pad = jnp.zeros((slab.shape[1] - side, LANES), F32)

    def store_group(g, carry):
        for k in range(GROUP):
            y = g * GROUP + k
            box = jnp.zeros((side, LANES), F32)
            for orb in range(orbs):
                q = even[y + 1, pl.ds(orbs + orb, side, stride=orbs), :] * scales[pl.ds(orb, 1), :]
                packed[pl.ds(orb * side, side), pl.ds(k * LANES, LANES)] = q.astype(BF16)
                box = box + q * q
            box = box * sign
            box = box + pltpu.roll(box, HALF, axis=1)
            slab[y + own_y] = pltpu.roll(jnp.concatenate([box, pad], 0), own_x, axis=0)
        base = g * (GROUP * side)
        for tile in range(3):
            flat = None
            for index, (pair, t) in enumerate(TILES):
                if t == tile:
                    term = dot(packed[:, pl.ds(2 * pair * LANES, 2 * LANES)], moves[index])
                    flat = term if flat is None else flat + term
            cols = pl.ds(pl.multiple_of(base + tile * LANES, LANES), LANES)
            for f in range(2):
                out_ref[f, :, :, cols] = (
                    flat[:, f * LANES : (f + 1) * LANES].astype(BF16).reshape(orbs, side, LANES)
                )
        return carry

    lax.fori_loop(0, groups, store_group, 0)

    cut = lane[:8]

    def pack(i, carry):
        for j in range(reach[1]):
            target = (row_index + i) % mesh_sizes[0] * mesh_sizes[1]
            target = target + (col_index + j) % mesh_sizes[1]
            for part in range(reach[2] // 8):
                xs = pl.ds(pl.multiple_of(i * reach[2] + part * 8, 8), 8)
                v = []
                for k in range(GROUP):
                    line = slab[j * GROUP + k, xs, :]
                    shift = k * side % LANES
                    v.append(line if shift == 0 else pltpu.roll(line, shift, axis=1))
                tiles = (
                    jnp.where(cut < 48, v[0], jnp.where(cut < 96, v[1], v[2])),
                    jnp.where(
                        cut < 16, v[2], jnp.where(cut < 64, v[3], jnp.where(cut < 112, v[4], v[5]))
                    ),
                    jnp.where(cut < 32, v[5], jnp.where(cut < 80, v[6], v[7])),
                )
                for t in range(3):
                    send_ref[target, pl.ds((part * 3 + t) * 8, 8), :] = tiles[t]
        return carry

    lax.fori_loop(0, reach[0], pack, 0)


def gather_kernel(reach, mesh_sizes, own, side, starts_ref, got_ref, high_ref, low_ref, dens_ref, spec_ref, acc):
    row_index, col_index = own()
    acc[...] = jnp.zeros_like(acc)
    depth = acc.shape[0]
    lane = lax.broadcasted_iota(jnp.int32, (8, LANES), 1)

    def add(step, carry):
        i = step // reach[1]
        j = step % reach[1]
        source = (row_index + mesh_sizes[0] - i) % mesh_sizes[0] * mesh_sizes[1]
        source = source + (col_index + mesh_sizes[1] - j) % mesh_sizes[1]
        start = starts_ref[source]
        tile = start // LANES
        inner = start % LANES
        following = (tile + 1) % depth
        here = (lane >= inner) & (lane < inner + side)
        wrapped = lane < inner + side - LANES
        for part in range(reach[2] // 8):
            t0, t1, t2 = (got_ref[source, pl.ds((part * 3 + t) * 8, 8), :] for t in range(3))
            joined = (
                t0, t0, jnp.where(lane >= 96, t0, t1), t1, t1, jnp.where(lane >= 112, t1, t2), t2, t2
            )
            for k in range(GROUP):
                moved = pltpu.roll(joined[k], (inner + (LANES - k * side % LANES)) % LANES, axis=1)
                rows = pl.ds(part * 64 + k, 8, stride=GROUP)
                acc[tile, rows, :] += jnp.where(here, moved, 0.0)
                acc[following, rows, :] += jnp.where(wrapped, moved, 0.0)
        return carry

    lax.fori_loop(0, reach[0] * reach[1], add, 0)
    whole = jnp.concatenate([acc[t] for t in range(depth)], 1)
    dens_ref[...] = whole.reshape(dens_ref.shape)
    spec_ref[...] = dot3((high_ref[...], low_ref[...]), split2(whole), ((1,), (1,)))


def screen_kernel(rows, cols, own, sizes, got_ref, vh, vl, wh, wl, out_ref):
    row_index, col_index = own()
    thin = got_ref.shape[1]
    nx, ny, nz = sizes
    cx, cy = nx // rows, ny // cols
    v = (vh[...], vl[...])
    w = (wh[...], wl[...])
    by_x = jnp.concatenate(
        [jnp.concatenate([got_ref[r * cols + c] for r in range(rows)], 1) for c in range(cols)], 0
    )
    by_x = dot3(split2(by_x), v)
    by_y = jnp.concatenate(
        [
            jnp.concatenate(
                [
                    by_x[c * thin : (c + 1) * thin, r * LANES : (r + 1) * LANES]
                    for c in range(cols)
                ],
                1,
            )
            for r in range(rows)
        ],
        0,
    )
    by_y = dot3(split2(by_y), w)

    def square(index, length):
        signed = jnp.where(index <= length // 2, index, index - length).astype(F32)
        wave = signed * (2 * math.pi / length)
        return wave * wave

    row = lax.broadcasted_iota(jnp.int32, by_y.shape, 0)
    lane = lax.broadcasted_iota(jnp.int32, by_y.shape, 1)
    kz = (row_index * cols + col_index) * thin + row % thin
    kx = row // thin * cx + lane % LANES // cy
    ky = lane // LANES * cy + lane % cy
    k_square = (square(kx, nx) + square(ky, ny)) + square(kz, nz)
    factor = jnp.where(k_square > 0, SCREEN / (k_square + SCREEN), 0.0)
    by_y = dot3(split2(by_y * factor), w, ((1,), (1,)))
    by_x = jnp.concatenate(
        [
            jnp.concatenate(
                [
                    by_y[r * thin : (r + 1) * thin, c * LANES : (c + 1) * LANES]
                    for r in range(rows)
                ],
                1,
            )
            for c in range(cols)
        ],
        0,
    )
    by_x = dot3(split2(by_x), v, ((1,), (1,)))
    for r in range(rows):
        for c in range(cols):
            out_ref[r * cols + c] = by_x[c * thin : (c + 1) * thin, r * LANES : (r + 1) * LANES]


def back_kernel(got_ref, high_ref, low_ref, out_ref):
    spec = jnp.transpose(got_ref[...], (1, 0))
    out_ref[...] = dot3(split2(spec), (high_ref[...], low_ref[...])).reshape(out_ref.shape)


def shards(orbitals, potential_boxes, corners, signs, counts, *, rows, cols, out_block):
    cx, cy, nz = out_block
    frags, orbs, side, _ = orbitals.shape
    peers = rows * cols
    nx, ny = cx * rows, cy * cols
    thin = nz // peers
    reach = ((cx + side - 2) // cx + 1, (cy + side - 2) // cy + 1, cx, cy)
    mesh_sizes = (rows, cols)

    def own():
        return lax.axis_index("row"), lax.axis_index("col")

    vmem = pl.BlockSpec(memory_space=pltpu.VMEM)
    smem = pl.BlockSpec(memory_space=pltpu.SMEM)
    params = pltpu.CompilerParams(vmem_limit_bytes=52 * 2**20)
    starts = lax.all_gather(corners[0, 2], ("row", "col"))
    block_rows = cx // 8 * 3 * 8
    filtered, send = pl.pallas_call(
        functools.partial(filter_kernel, reach, mesh_sizes, own),
        out_shape=(
            jax.ShapeDtypeStruct(orbitals.shape, BF16),
            jax.ShapeDtypeStruct((peers, block_rows, LANES), F32),
        ),
        in_specs=[smem] * 3 + [vmem] * 2,
        out_specs=(vmem, vmem),
        scratch_shapes=[
            pltpu.VMEM((side + 2, (side + 2) * orbs, LANES), F32),
            pltpu.VMEM((side + 2, (side + 2) * orbs, LANES), F32),
            pltpu.VMEM((side, side, LANES), F32),
            pltpu.VMEM((len(TILES), 2 * LANES, 2 * LANES), BF16),
            pltpu.VMEM((orbs * side, GROUP * LANES), BF16),
            pltpu.VMEM((reach[1] * cy, reach[0] * cx, LANES), F32),
            pltpu.VMEM((orbs, LANES), F32),
        ],
        compiler_params=params,
    )(corners, signs, counts, orbitals, potential_boxes)
    got = lax.all_to_all(send, ("row", "col"), 0, 0, tiled=True)
    z_high, z_low = split_table(real_basis(nz))
    density, spec = pl.pallas_call(
        functools.partial(gather_kernel, reach, mesh_sizes, own, side),
        out_shape=(
            jax.ShapeDtypeStruct(out_block, F32),
            jax.ShapeDtypeStruct((nz, cx * cy), F32),
        ),
        in_specs=[smem] + [vmem] * 3,
        out_specs=(vmem, vmem),
        scratch_shapes=[pltpu.VMEM((nz // LANES, cx * cy, LANES), F32)],
        compiler_params=params,
    )(starts, got, z_high, z_low)
    spec = spec.reshape(peers, thin, cx * cy)
    spec = lax.all_to_all(spec, ("row", "col"), 0, 0, tiled=True)
    x_basis, y_basis = real_basis(nx), real_basis(ny)
    if thin % 8 == 0 and ny * cx <= 1024:
        x_table = np.kron(x_basis.T, np.eye(cy))
        y_table = np.einsum("mcy,xw->cxymw", y_basis.reshape(ny, cols, cy), np.eye(cx))
        y_table = y_table.reshape(cols * cx * cy, cols, cy, cx).transpose(0, 1, 3, 2)
        y_table = y_table.reshape(cols * cx * cy, cols * cx * cy)
        spec = pl.pallas_call(
            functools.partial(screen_kernel, rows, cols, own, (nx, ny, nz)),
            out_shape=jax.ShapeDtypeStruct(spec.shape, F32),
            in_specs=[vmem] * 5,
            out_specs=vmem,
            compiler_params=params,
        )(spec, *split_table(x_table), *split_table(y_table))
    else:
        x_basis, y_basis = x_basis.astype(np.float32), y_basis.astype(np.float32)

        def square(index, length):
            wave = jnp.where(index <= length // 2, index, index - length).astype(F32) * (
                2 * math.pi / length
            )
            return wave * wave

        r, c = own()
        grid = spec.reshape(rows, cols, thin, cx, cy).transpose(2, 0, 3, 1, 4)
        grid = grid.reshape(thin, nx, ny)
        grid = jnp.einsum("kxy,ax,by->kab", grid, x_basis, y_basis, precision=HIGHEST)
        k_square = (
            square(jnp.arange(nx), nx)[None, :, None] + square(jnp.arange(ny), ny)[None, None, :]
        ) + square((r * cols + c) * thin + jnp.arange(thin), nz)[:, None, None]
        grid = grid * jnp.where(k_square > 0, SCREEN / (k_square + SCREEN), 0.0)
        grid = jnp.einsum("kab,ax,by->kxy", grid, x_basis, y_basis, precision=HIGHEST)
        grid = grid.reshape(thin, rows, cx, cols, cy).transpose(1, 3, 0, 2, 4)
        spec = grid.reshape(spec.shape)
    spec = lax.all_to_all(spec, ("row", "col"), 0, 0, tiled=True).reshape(nz, cx * cy)
    hartree = pl.pallas_call(
        back_kernel,
        out_shape=jax.ShapeDtypeStruct(out_block, F32),
        in_specs=[vmem] * 3,
        out_specs=vmem,
        compiler_params=params,
    )(spec, z_high, z_low)
    return (filtered, density, hartree)


def solution(mesh):
    rows, cols = mesh.shape["row"], mesh.shape["col"]
    return jax.shard_map(
        functools.partial(shards, rows=rows, cols=cols, out_block=(16, 8, 512)),
        mesh=mesh,
        in_specs=(
            P(("row", "col"), None, None, None),
            P(("row", "col"), None, None),
            P(("row", "col"), None),
            P(("row", "col")),
            P(("row", "col")),
        ),
        out_specs=(
            P(("row", "col"), None, None, None),
            P("row", "col", None),
            P("row", "col", None),
        ),
        check_vma=False,
    )
```

```python
import functools
import math

import jax
import jax.numpy as jnp
import ml_dtypes
import numpy as np
from jax import lax
from jax.experimental import pallas as pl
from jax.experimental.pallas import tpu as pltpu
from jax.sharding import PartitionSpec as P

CENTER = 5.25
HALF_WIDTH = 3.75
SCREEN = 0.0025
LANES = 128
HALF = 64
PLANES = 4
GROUP = 8
HIGHEST = lax.Precision.HIGHEST
BF16 = jnp.bfloat16
F32 = jnp.float32
MESH = pl.DeviceIdType.MESH
TILES = ((0, 0), (1, 0), (1, 1), (2, 1), (2, 2), (3, 2))


def real_basis(length):
    m = np.arange(length)[:, None]
    n = np.arange(length)[None, :]
    angle = 2 * np.pi * ((m * n) % length) / length
    rows = np.where(m <= length // 2, np.cos(angle), np.sin(angle))
    weight = np.where((m == 0) | (2 * m == length), 1.0, 2.0) / length
    return rows * np.sqrt(weight)


def split_table(table):
    high = table.astype(np.float32).astype(ml_dtypes.bfloat16)
    low = (table - high.astype(np.float64)).astype(np.float32).astype(ml_dtypes.bfloat16)
    return high, low


def split2(value):
    high = value.astype(BF16)
    return high, (value - high.astype(F32)).astype(BF16)


def dot(a, b, dims=((1,), (0,))):
    return lax.dot_general(a, b, (dims, ((), ())), preferred_element_type=F32)


def dot3(a, b, dims=((1,), (0,))):
    return dot(a[0], b[0], dims) + (dot(a[0], b[1], dims) + dot(a[1], b[0], dims))


def move_matrix(pair, tile, side, inward):
    shape = (2 * LANES, 2 * LANES)
    boxed = lax.broadcasted_iota(jnp.int32, shape, 1 if inward else 0)
    flat = lax.broadcasted_iota(jnp.int32, shape, 0 if inward else 1)
    y = 2 * pair + boxed // LANES
    fragment = boxed % LANES // HALF
    z = boxed % HALF
    hit = (fragment == flat // LANES) & (z < side)
    hit = hit & (y * side + z == tile * LANES + flat % LANES)
    return jnp.where(hit, 1.0, 0.0).astype(BF16)


def filter_kernel(
    reach,
    own,
    corners_ref,
    signs_ref,
    counts_ref,
    orb_ref,
    pot_ref,
    out_ref,
    send_ref,
    even,
    odd,
    coef,
    moves,
    packed,
    slab,
    scales,
):
    _, orbs, side, _ = orb_ref.shape
    rows = orbs * side
    groups = side // GROUP
    lane = lax.broadcasted_iota(jnp.int32, (orbs, LANES), 1)
    for index, (pair, tile) in enumerate(TILES):
        moves[index] = move_matrix(pair, tile, side, True)
    for field in (even, odd):
        zeros = jnp.zeros((field.shape[1], LANES), F32)
        field[0] = zeros
        field[side + 1] = zeros
        edge = jnp.zeros((orbs, LANES), F32)

        def clear(y, carry):
            field[y, pl.ds(0, orbs), :] = edge
            field[y, pl.ds(orbs * (side + 1), orbs), :] = edge
            return carry

        lax.fori_loop(1, side + 1, clear, 0)

    def spread(parts):
        results = []
        for pair in range(GROUP // 2):
            total = None
            for index, (p, tile) in enumerate(TILES):
                if p == pair:
                    term = dot(parts[tile], moves[index])
                    total = term if total is None else total + term
            results.append(total)
        return results

    def load_group(g, carry):
        base = g * (GROUP * side)
        parts = []
        pot_parts = []
        for tile in range(3):
            cols = pl.ds(pl.multiple_of(base + tile * LANES, LANES), LANES)
            parts.append(
                jnp.concatenate([orb_ref[f, :, :, cols].reshape(rows, LANES) for f in range(2)], 1)
            )
            pot = jnp.concatenate([pot_ref[f, :, cols] for f in range(2)], 1)
            first = pot.astype(BF16)
            rest = pot - first.astype(F32)
            second = rest.astype(BF16)
            third = (rest - second.astype(F32)).astype(BF16)
            pot_parts.append(jnp.concatenate([first, second, third], 0))
        fields = spread(parts)
        pots = spread(pot_parts)
        for pair in range(GROUP // 2):
            for k in range(2):
                y = g * GROUP + 2 * pair + k
                cols = slice(k * LANES, (k + 1) * LANES)
                for orb in range(orbs):
                    even[y + 1, pl.ds(orbs + orb, side, stride=orbs), :] = fields[pair][
                        orb * side : (orb + 1) * side, cols
                    ]
                stack = pots[pair][:, cols]
                pot = (stack[:side] + stack[side : 2 * side]) + stack[2 * side :]
                coef[y] = (pot + (3.0 - CENTER)) * (2.0 / HALF_WIDTH)
        return carry

    lax.fori_loop(0, groups, load_group, 0)

    coupling = jnp.where(lane % HALF < side, 1.0 / HALF_WIDTH, 0.0).astype(F32)

    def step(now, other, first, last):
        def planes(group, total):
            top = group * PLANES + 1
            squares = None
            before = [now[top + k, pl.ds(0, orbs), :] for k in range(PLANES)]
            here = [now[top + k, pl.ds(orbs, orbs), :] for k in range(PLANES)]
            for x in range(side):
                row = pl.ds(orbs * (x + 1), orbs)
                after = [now[top + k, pl.ds(orbs * (x + 2), orbs), :] for k in range(PLANES)]
                column = [now[top - 1, row, :]] + here + [now[top + PLANES, row, :]]
                for k in range(PLANES):
                    beside = (before[k] + after[k]) + (column[k] + column[k + 2])
                    beside = beside + (
                        pltpu.roll(here[k], 1, axis=1) + pltpu.roll(here[k], LANES - 1, axis=1)
                    )
                    result = coef[top + k - 1, pl.ds(x, 1), :] * here[k] - coupling * beside
                    result = 0.5 * result if first else result - other[top + k, row, :]
                    other[top + k, row, :] = result
                    if last:
                        square = result * result
                        squares = square if squares is None else squares + square
                before, here = here, after
            return total + squares if last else total

        return lax.fori_loop(0, side // PLANES, planes, jnp.zeros((orbs, LANES), F32))

    step(even, odd, True, False)
    step(odd, even, False, False)
    step(even, odd, False, False)
    step(odd, even, False, False)
    step(even, odd, False, False)
    total = step(odd, even, False, True)

    left = lane < HALF
    sums = jnp.where(
        left,
        jnp.sum(jnp.where(left, total, 0.0), axis=1, keepdims=True),
        jnp.sum(jnp.where(left, 0.0, total), axis=1, keepdims=True),
    )
    shifted = sums * (1.0 / side**3) + 1e-6
    scale = lax.rsqrt(shifted)
    scale = scale * (1.5 - 0.5 * shifted * scale * scale)
    live = lax.broadcasted_iota(jnp.int32, (orbs, LANES), 0) < jnp.where(
        left, counts_ref[0], counts_ref[1]
    )
    scales[...] = jnp.where(live, scale, 0.0)
    sign = jnp.where(left, signs_ref[0], signs_ref[1]).astype(F32)[:1]

    for index, (pair, tile) in enumerate(TILES):
        moves[index] = move_matrix(pair, tile, side, False)
    row_index, col_index = own()
    own_x = corners_ref[0, 0] - row_index * reach[2]
    own_y = corners_ref[0, 1] - col_index * reach[3]
    slab[...] = jnp.zeros_like(slab)
    pad = jnp.zeros((slab.shape[1] - side, LANES), F32)

    def store_group(g, carry):
        for k in range(GROUP):
            y = g * GROUP + k
            box = jnp.zeros((side, LANES), F32)
            for orb in range(orbs):
                q = even[y + 1, pl.ds(orbs + orb, side, stride=orbs), :] * scales[pl.ds(orb, 1), :]
                packed[pl.ds(orb * side, side), pl.ds(k * LANES, LANES)] = q.astype(BF16)
                box = box + q * q
            box = box * sign
            box = box + pltpu.roll(box, HALF, axis=1)
            slab[y + own_y] = pltpu.roll(jnp.concatenate([box, pad], 0), own_x, axis=0)
        base = g * (GROUP * side)
        for tile in range(3):
            flat = None
            for index, (pair, t) in enumerate(TILES):
                if t == tile:
                    term = dot(packed[:, pl.ds(2 * pair * LANES, 2 * LANES)], moves[index])
                    flat = term if flat is None else flat + term
            cols = pl.ds(pl.multiple_of(base + tile * LANES, LANES), LANES)
            for f in range(2):
                out_ref[f, :, :, cols] = (
                    flat[:, f * LANES : (f + 1) * LANES].astype(BF16).reshape(orbs, side, LANES)
                )
        return carry

    lax.fori_loop(0, groups, store_group, 0)

    cut = lane[:8]

    start = jnp.full((8, LANES), corners_ref[0, 2], jnp.int32).astype(F32)

    def pack(i, carry):
        for j in range(reach[1]):
            slot = i * reach[1] + j
            for part in range(reach[2] // 8):
                xs = pl.ds(pl.multiple_of(i * reach[2] + part * 8, 8), 8)
                v = []
                for k in range(GROUP):
                    line = slab[j * GROUP + k, xs, :]
                    shift = k * side % LANES
                    v.append(line if shift == 0 else pltpu.roll(line, shift, axis=1))
                tiles = (
                    jnp.where(cut < 48, v[0], jnp.where(cut < 96, v[1], v[2])),
                    jnp.where(
                        cut < 16, v[2], jnp.where(cut < 64, v[3], jnp.where(cut < 112, v[4], v[5]))
                    ),
                    jnp.where(cut < 32, v[5], jnp.where(cut < 80, v[6], v[7])),
                )
                for t in range(3):
                    send_ref[slot, pl.ds((part * 3 + t) * 8, 8), :] = tiles[t]
            send_ref[slot, pl.ds(reach[2] * 3, 8), :] = start
        return carry

    lax.fori_loop(0, reach[0], pack, 0)


def halo_kernel(reach, mesh_sizes, own, send_ref, got_ref, send_sems, recv_sems, local_sem):
    row_index, col_index = own()
    rows, cols = mesh_sizes
    barrier = pltpu.get_barrier_semaphore()
    offsets = [(i, j) for i in range(reach[0]) for j in range(reach[1])][1:]
    for i, j in offsets:
        source = ((row_index + rows - i) % rows, (col_index + cols - j) % cols)
        pl.semaphore_signal(barrier, inc=1, device_id=source, device_id_type=MESH)
    pl.semaphore_wait(barrier, len(offsets))
    copies = []
    for i, j in offsets:
        slot = i * reach[1] + j
        copy = pltpu.make_async_remote_copy(
            src_ref=send_ref.at[slot],
            dst_ref=got_ref.at[slot],
            send_sem=send_sems.at[slot],
            recv_sem=recv_sems.at[slot],
            device_id=((row_index + i) % rows, (col_index + j) % cols),
            device_id_type=MESH,
        )
        copy.start()
        copies.append(copy)
    local = pltpu.make_async_copy(send_ref.at[0], got_ref.at[0], local_sem)
    local.start()
    local.wait()
    for copy in copies:
        copy.wait()


def gather_kernel(reach, side, starts_ref, got_ref, high_ref, low_ref, dens_ref, spec_ref, acc):
    acc[...] = jnp.zeros_like(acc)
    depth = acc.shape[0]
    lane = lax.broadcasted_iota(jnp.int32, (8, LANES), 1)

    def add(source, carry):
        start = starts_ref[source]
        tile = start // LANES
        inner = start % LANES
        following = (tile + 1) % depth
        here = (lane >= inner) & (lane < inner + side)
        wrapped = lane < inner + side - LANES
        for part in range(reach[2] // 8):
            t0, t1, t2 = (got_ref[source, pl.ds((part * 3 + t) * 8, 8), :] for t in range(3))
            joined = (
                t0, t0, jnp.where(lane >= 96, t0, t1), t1, t1, jnp.where(lane >= 112, t1, t2), t2, t2
            )
            for k in range(GROUP):
                moved = pltpu.roll(joined[k], (inner + (LANES - k * side % LANES)) % LANES, axis=1)
                rows = pl.ds(part * 64 + k, 8, stride=GROUP)
                acc[tile, rows, :] += jnp.where(here, moved, 0.0)
                acc[following, rows, :] += jnp.where(wrapped, moved, 0.0)
        return carry

    lax.fori_loop(0, reach[0] * reach[1], add, 0)
    whole = jnp.concatenate([acc[t] for t in range(depth)], 1)
    dens_ref[...] = whole.reshape(dens_ref.shape)
    spec_ref[...] = dot3((high_ref[...], low_ref[...]), split2(whole), ((1,), (1,)))


def screen_kernel(
    rows, cols, own, sizes, spec_ref, vh, vl, wh, wl, zh, zl, hart_ref, got_ref, out_ref, back_ref,
    send_sems, recv_sems,
):
    row_index, col_index = own()
    me = row_index * cols + col_index
    peers = rows * cols
    barrier = pltpu.get_barrier_semaphore()

    def device(offset):
        other = (me + offset) % peers
        return other, (other // cols, other % cols)

    def greet(offset, carry):
        pl.semaphore_signal(barrier, inc=1, device_id=device(offset)[1], device_id_type=MESH)
        return carry

    def exchange(source_ref, target_ref, phase):
        def copy(offset):
            other, where = device(offset)
            return pltpu.make_async_remote_copy(
                src_ref=source_ref.at[other],
                dst_ref=target_ref.at[me],
                send_sem=send_sems.at[phase, offset],
                recv_sem=recv_sems.at[phase, offset],
                device_id=where,
                device_id_type=MESH,
            )

        def start(offset, carry):
            copy(offset).start()
            return carry

        def finish(offset, carry):
            copy(offset).wait()
            return carry

        lax.fori_loop(1, peers, start, 0)
        target_ref[me] = source_ref[me]
        lax.fori_loop(1, peers, finish, 0)

    lax.fori_loop(1, peers, greet, 0)
    pl.semaphore_wait(barrier, peers - 1)
    exchange(spec_ref, got_ref, 0)
    thin = got_ref.shape[1]
    nx, ny, nz = sizes
    cx, cy = nx // rows, ny // cols
    v = (vh[...], vl[...])
    w = (wh[...], wl[...])
    by_x = jnp.concatenate(
        [jnp.concatenate([got_ref[r * cols + c] for r in range(rows)], 1) for c in range(cols)], 0
    )
    by_x = dot3(split2(by_x), v)
    by_y = jnp.concatenate(
        [
            jnp.concatenate(
                [
                    by_x[c * thin : (c + 1) * thin, r * LANES : (r + 1) * LANES]
                    for c in range(cols)
                ],
                1,
            )
            for r in range(rows)
        ],
        0,
    )
    by_y = dot3(split2(by_y), w)

    def square(index, length):
        signed = jnp.where(index <= length // 2, index, index - length).astype(F32)
        wave = signed * (2 * math.pi / length)
        return wave * wave

    row = lax.broadcasted_iota(jnp.int32, by_y.shape, 0)
    lane = lax.broadcasted_iota(jnp.int32, by_y.shape, 1)
    kz = (row_index * cols + col_index) * thin + row % thin
    kx = row // thin * cx + lane % LANES // cy
    ky = lane // LANES * cy + lane % cy
    k_square = (square(kx, nx) + square(ky, ny)) + square(kz, nz)
    factor = jnp.where(k_square > 0, SCREEN / (k_square + SCREEN), 0.0)
    by_y = dot3(split2(by_y * factor), w, ((1,), (1,)))
    by_x = jnp.concatenate(
        [
            jnp.concatenate(
                [
                    by_y[r * thin : (r + 1) * thin, c * LANES : (c + 1) * LANES]
                    for r in range(rows)
                ],
                1,
            )
            for c in range(cols)
        ],
        0,
    )
    by_x = dot3(split2(by_x), v, ((1,), (1,)))
    for r in range(rows):
        for c in range(cols):
            out_ref[r * cols + c] = by_x[c * thin : (c + 1) * thin, r * LANES : (r + 1) * LANES]
    exchange(out_ref, back_ref, 1)
    back = back_ref[...].reshape(peers * thin, LANES)
    to_cells(back, zh, zl, hart_ref)


def to_cells(spec, high_ref, low_ref, out_ref):
    spec = jnp.transpose(spec, (1, 0))
    out_ref[...] = dot3(split2(spec), (high_ref[...], low_ref[...])).reshape(out_ref.shape)


def back_kernel(got_ref, high_ref, low_ref, out_ref):
    to_cells(got_ref[...], high_ref, low_ref, out_ref)


def shards(orbitals, potential_boxes, corners, signs, counts, *, rows, cols, out_block):
    cx, cy, nz = out_block
    frags, orbs, side, _ = orbitals.shape
    peers = rows * cols
    nx, ny = cx * rows, cy * cols
    thin = nz // peers
    reach = ((cx + side - 2) // cx + 1, (cy + side - 2) // cy + 1, cx, cy)
    mesh_sizes = (rows, cols)

    def own():
        return lax.axis_index("row"), lax.axis_index("col")

    vmem = pl.BlockSpec(memory_space=pltpu.VMEM)
    smem = pl.BlockSpec(memory_space=pltpu.SMEM)
    params = pltpu.CompilerParams(vmem_limit_bytes=52 * 2**20)
    slots = reach[0] * reach[1]
    block = jax.ShapeDtypeStruct((slots, cx * 3 + 8, LANES), F32)
    filtered, send = pl.pallas_call(
        functools.partial(filter_kernel, reach, own),
        out_shape=(
            jax.ShapeDtypeStruct(orbitals.shape, BF16),
            block,
        ),
        in_specs=[smem] * 3 + [vmem] * 2,
        out_specs=(vmem, vmem),
        scratch_shapes=[
            pltpu.VMEM((side + 2, (side + 2) * orbs, LANES), F32),
            pltpu.VMEM((side + 2, (side + 2) * orbs, LANES), F32),
            pltpu.VMEM((side, side, LANES), F32),
            pltpu.VMEM((len(TILES), 2 * LANES, 2 * LANES), BF16),
            pltpu.VMEM((orbs * side, GROUP * LANES), BF16),
            pltpu.VMEM((reach[1] * cy, reach[0] * cx, LANES), F32),
            pltpu.VMEM((orbs, LANES), F32),
        ],
        compiler_params=params,
    )(corners, signs, counts, orbitals, potential_boxes)
    got = pl.pallas_call(
        functools.partial(halo_kernel, reach, mesh_sizes, own),
        out_shape=block,
        in_specs=[vmem],
        out_specs=vmem,
        scratch_shapes=[
            pltpu.SemaphoreType.DMA((slots,)),
            pltpu.SemaphoreType.DMA((slots,)),
            pltpu.SemaphoreType.DMA,
        ],
        compiler_params=pltpu.CompilerParams(collective_id=0, has_side_effects=True),
    )(send)
    starts = got[:, cx * 3, 0].astype(jnp.int32)
    z_high, z_low = split_table(real_basis(nz))
    density, spec = pl.pallas_call(
        functools.partial(gather_kernel, reach, side),
        out_shape=(
            jax.ShapeDtypeStruct(out_block, F32),
            jax.ShapeDtypeStruct((nz, cx * cy), F32),
        ),
        in_specs=[smem] + [vmem] * 3,
        out_specs=(vmem, vmem),
        scratch_shapes=[pltpu.VMEM((nz // LANES, cx * cy, LANES), F32)],
        compiler_params=params,
    )(starts, got, z_high, z_low)
    spec = spec.reshape(peers, thin, cx * cy)
    x_basis, y_basis = real_basis(nx), real_basis(ny)
    if thin % 8 == 0 and ny * cx <= 1024:
        x_table = np.kron(x_basis.T, np.eye(cy))
        y_table = np.einsum("mcy,xw->cxymw", y_basis.reshape(ny, cols, cy), np.eye(cx))
        y_table = y_table.reshape(cols * cx * cy, cols, cy, cx).transpose(0, 1, 3, 2)
        y_table = y_table.reshape(cols * cx * cy, cols * cx * cy)
        blocks = pltpu.VMEM(spec.shape, F32)
        hartree = pl.pallas_call(
            functools.partial(screen_kernel, rows, cols, own, (nx, ny, nz)),
            out_shape=jax.ShapeDtypeStruct(out_block, F32),
            in_specs=[vmem] * 7,
            out_specs=vmem,
            scratch_shapes=[
                blocks,
                blocks,
                blocks,
                pltpu.SemaphoreType.DMA((2, peers)),
                pltpu.SemaphoreType.DMA((2, peers)),
            ],
            compiler_params=pltpu.CompilerParams(
                collective_id=1, has_side_effects=True, vmem_limit_bytes=52 * 2**20
            ),
        )(spec, *split_table(x_table), *split_table(y_table), z_high, z_low)
    else:
        x_basis, y_basis = x_basis.astype(np.float32), y_basis.astype(np.float32)

        def square(index, length):
            wave = jnp.where(index <= length // 2, index, index - length).astype(F32) * (
                2 * math.pi / length
            )
            return wave * wave

        r, c = own()
        spec = lax.all_to_all(spec, ("row", "col"), 0, 0, tiled=True)
        grid = spec.reshape(rows, cols, thin, cx, cy).transpose(2, 0, 3, 1, 4)
        grid = grid.reshape(thin, nx, ny)
        grid = jnp.einsum("kxy,ax,by->kab", grid, x_basis, y_basis, precision=HIGHEST)
        k_square = (
            square(jnp.arange(nx), nx)[None, :, None] + square(jnp.arange(ny), ny)[None, None, :]
        ) + square((r * cols + c) * thin + jnp.arange(thin), nz)[:, None, None]
        grid = grid * jnp.where(k_square > 0, SCREEN / (k_square + SCREEN), 0.0)
        grid = jnp.einsum("kab,ax,by->kxy", grid, x_basis, y_basis, precision=HIGHEST)
        grid = grid.reshape(thin, rows, cx, cols, cy).transpose(1, 3, 0, 2, 4)
        spec = lax.all_to_all(grid.reshape(spec.shape), ("row", "col"), 0, 0, tiled=True)
        hartree = pl.pallas_call(
            back_kernel,
            out_shape=jax.ShapeDtypeStruct(out_block, F32),
            in_specs=[vmem] * 3,
            out_specs=vmem,
            compiler_params=params,
        )(spec.reshape(nz, cx * cy), z_high, z_low)
    return (filtered, density, hartree)


def solution(mesh):
    rows, cols = mesh.shape["row"], mesh.shape["col"]
    return jax.shard_map(
        functools.partial(shards, rows=rows, cols=cols, out_block=(16, 8, 512)),
        mesh=mesh,
        in_specs=(
            P(("row", "col"), None, None, None),
            P(("row", "col"), None, None),
            P(("row", "col"), None),
            P(("row", "col")),
            P(("row", "col")),
        ),
        out_specs=(
            P(("row", "col"), None, None, None),
            P("row", "col", None),
            P("row", "col", None),
        ),
        check_vma=False,
    )
```
